32 devices in a mesh: dp: 8 (over y, x, core), mp: 4 (over z).
Axes of the slice: x: 2, y: 2, z: 4, core: 2. Of those that a mesh axis runs over, the one named last changes fastest.
Arguments:
- query_rows: bfloat16 [2048, 6144], P('dp', 'mp'), may hold values from -6 to 6
- key_rows: bfloat16 [2048, 6144], P('dp', 'mp'), may hold values from -6 to 6
- value_rows: bfloat16 [2048, 6144], P('dp', 'mp'), may hold values from -6 to 6
- proj_weight: bfloat16 [6144, 6144], P('mp'), may hold values from -0.078125 to 0.078125
- out_grad: bfloat16 [2048, 6144], P('dp', 'mp'), may hold values from -6 to 6
- image_starts: int32 [8, 256], replicated, may hold values from -1 to 128, as said below
Outputs:
- projected: bfloat16 [2048, 6144], P('dp', 'mp')
- grad_query: bfloat16 [2048, 6144], P('dp', 'mp')
- grad_key: bfloat16 [2048, 6144], P('dp', 'mp')
- grad_value: bfloat16 [2048, 6144], P('dp', 'mp')
The draws below stay inside these ranges and needn't reach their ends.
Inputs may be any that keep to these rules, and one draw needn't show every extreme that they name: `image_starts`: each used row holds the index, within its pack, of the first row of its image; unused rows hold -1. A pack's used rows come first without gaps and its images are contiguous. Images begin only at rows 0, 64 and 128; one at 64 only in packs that use more than 128 rows. The data loader fills packs two at a time, splitting one batch of images between them, so packs t and t + 4 form a pair: one of them uses all of its first 128 rows, has an image beginning at row 128 that runs to its last used row, and uses some rows past it; the other uses fewer than 128 rows; together they use exactly 256 rows.
All inputs are finite; a program needn't handle non-finite values.
Results may differ from the reference program's by a relative error of at most 0.022.
Values may be sent and summed in bfloat16 or wider, within the bound.
A program may use at most 64 MiB of HBM per device.

```python
import math
import jax
import jax.numpy as jnp
from jax import lax

HEADS = 48
HEAD_DIM = 128
D = 6144
HEADS_DEV = 12
WORK_ROWS = 128
PACK_ROWS = 256
TOKENS = 2048
N_DP = 8
N_MP = 4


def pack_starts(key):
    key = jax.random.fold_in(key, 101)
    first_key, second_key, third_key = jax.random.split(key, 3)
    half_count = N_DP // 2
    heavy_lower = jax.random.randint(first_key, (half_count,), 0, 2)
    light_count = jax.random.randint(second_key, (half_count,), WORK_ROWS // 4, 3 * WORK_ROWS // 4 + 1)
    heavy_count = 2 * WORK_ROWS - light_count
    lower_count = jnp.where(heavy_lower == 1, heavy_count, light_count)
    upper_count = jnp.where(heavy_lower == 1, light_count, heavy_count)
    used_count = jnp.concatenate([lower_count, upper_count])
    positions = jnp.arange(PACK_ROWS, dtype=jnp.int32)
    middle_coin = jax.random.randint(third_key, (N_DP,), 0, 2) == 1
    middle_flags = (middle_coin & (used_count > WORK_ROWS))[:, None] & (positions[None, :] == WORK_ROWS // 2)
    boundary_flags = middle_flags | (positions[None, :] == 0) | (positions[None, :] == WORK_ROWS)
    boundary_marks = jnp.where(boundary_flags, positions[None, :], -1)
    running_starts = lax.cummax(boundary_marks, axis=1)
    return jnp.where(positions[None, :] < used_count[:, None], running_starts, -1).astype(jnp.int32)


def draw_image_starts(key, part):
    return pack_starts(key)


def draw_query_rows(key, part):
    key = jax.random.fold_in(key, 5)
    first_key = jax.random.fold_in(key, 0)
    samples = jax.random.truncated_normal(first_key, -6.0, 6.0, (TOKENS, HEADS, HEAD_DIM), jnp.float32)
    return samples.reshape(TOKENS, HEADS * HEAD_DIM).astype(jnp.bfloat16)


def draw_key_rows(key, part):
    key = jax.random.fold_in(key, 7)
    first_key = jax.random.fold_in(key, 0)
    samples = jax.random.truncated_normal(first_key, -6.0, 6.0, (TOKENS, HEADS, HEAD_DIM), jnp.float32)
    return samples.reshape(TOKENS, HEADS * HEAD_DIM).astype(jnp.bfloat16)


def block_scale(rng, extent, cuts, low, largest):
    level, own = 1.0, jax.random.fold_in(rng, 6)
    for axis_at, blocks in cuts:
        draws = jnp.exp(jax.random.uniform(jax.random.fold_in(own, axis_at), (blocks,), jnp.float32, low / len(cuts), largest / len(cuts)))
        level = level * jnp.repeat(draws, extent[axis_at] // blocks).reshape([-1 if axis == axis_at else 1 for axis in range(len(extent))])
    return level


def gaussian(key, extent, deviation, reach, pieces=(), held_as=jnp.bfloat16):
    values = deviation * jax.random.normal(key, extent, jnp.float32)
    if pieces:
        values = values * block_scale(key, extent, pieces, -0.22, 0.18)
    return jnp.clip(values, -reach, reach).astype(held_as)


def setup_inputs(seed: int = 0) -> dict:
    keys = jax.random.split(jax.random.key(seed), 7)
    query_rows = draw_query_rows(jax.random.fold_in(keys[6], 71), 0)
    key_rows = draw_key_rows(jax.random.fold_in(keys[6], 71), 0)
    value_rows = gaussian(keys[2], (TOKENS, D), 1.0, 6.0, ((0, 8), (1, 4)))
    proj_weight = gaussian(keys[3], (D, D), D ** -0.5, 0.078125, ((0, 4),))
    out_grad = gaussian(keys[4], (TOKENS, D), 1.0, 6.0, ((0, 8), (1, 4)))
    image_starts = draw_image_starts(jax.random.fold_in(keys[6], 71), 0)
    return {"query_rows": query_rows, "key_rows": key_rows, "value_rows": value_rows, "proj_weight": proj_weight, "out_grad": out_grad, "image_starts": image_starts}


def pack_forward_backward(inputs, proj_weight):
    query_rows, key_rows, value_rows, out_grad, starts = inputs
    root_dim = math.sqrt(HEAD_DIM)
    query_heads = query_rows.astype(jnp.float32).reshape(PACK_ROWS, HEADS, HEAD_DIM)
    key_heads = key_rows.astype(jnp.float32).reshape(PACK_ROWS, HEADS, HEAD_DIM)
    value_heads = value_rows.astype(jnp.float32).reshape(PACK_ROWS, HEADS, HEAD_DIM)
    same_image = starts[:, None] == starts[None, :]
    valid_rows = (starts >= 0)[:, None]
    scores = jnp.einsum('qhd,khd->hqk', query_heads, key_heads) / root_dim
    scores = jnp.where(same_image[None], scores, -jnp.inf)
    maxima = lax.optimization_barrier(jnp.max(scores, axis=2, keepdims=True))
    weights = jnp.exp(scores - maxima)
    probabilities = weights / lax.optimization_barrier(jnp.sum(weights, axis=2, keepdims=True))
    rounded = lax.optimization_barrier(probabilities.astype(jnp.bfloat16)).astype(jnp.float32)
    attended = jnp.einsum('hqk,khd->qhd', rounded, value_heads).reshape(PACK_ROWS, D)
    attended = jnp.where(valid_rows, attended, 0.0).astype(jnp.bfloat16)
    grouped = attended.astype(jnp.float32).reshape(PACK_ROWS, N_MP, HEADS_DEV * HEAD_DIM)
    weight_groups = proj_weight.astype(jnp.float32).reshape(N_MP, HEADS_DEV * HEAD_DIM, D)
    partials = jnp.einsum('tgc,gcd->gtd', grouped, weight_groups)
    partials = lax.optimization_barrier(partials.astype(jnp.bfloat16)).astype(jnp.float32)
    projected = lax.optimization_barrier(jnp.sum(partials, axis=0)).astype(jnp.bfloat16)
    grad_attended = lax.dot_general(out_grad, proj_weight, (((1,), (1,)), ((), ())), preferred_element_type=jnp.float32).astype(jnp.bfloat16)
    grad_heads = grad_attended.astype(jnp.float32).reshape(PACK_ROWS, HEADS, HEAD_DIM)
    grad_value = jnp.einsum('hqk,qhd->khd', rounded, grad_heads)
    grad_weights = jnp.einsum('qhd,khd->hqk', grad_heads, value_heads)
    correction = lax.optimization_barrier(jnp.sum(probabilities * grad_weights, axis=2, keepdims=True))
    grad_scores = probabilities * (grad_weights - correction) / root_dim
    grad_scores = lax.optimization_barrier(grad_scores.astype(jnp.bfloat16)).astype(jnp.float32)
    grad_query = jnp.einsum('hqk,khd->qhd', grad_scores, key_heads)
    grad_key = jnp.einsum('hqk,qhd->khd', grad_scores, query_heads)

    def finish(gradient):
        return jnp.where(valid_rows, gradient.reshape(PACK_ROWS, D), 0.0).astype(jnp.bfloat16)
    return (projected, finish(grad_query), finish(grad_key), finish(grad_value))

def reference(query_rows, key_rows, value_rows, proj_weight, out_grad, image_starts):

    def per_pack(inputs):
        return pack_forward_backward(inputs, proj_weight)
    packed = (query_rows.reshape(N_DP, PACK_ROWS, D), key_rows.reshape(N_DP, PACK_ROWS, D), value_rows.reshape(N_DP, PACK_ROWS, D), out_grad.reshape(N_DP, PACK_ROWS, D), image_starts)
    projected, grad_query, grad_key, grad_value = lax.map(per_pack, packed)
    return (projected.reshape(TOKENS, D), grad_query.reshape(TOKENS, D), grad_key.reshape(TOKENS, D), grad_value.reshape(TOKENS, D))
```

```python
import math

import jax
import jax.numpy as jnp
from jax import lax
from jax.sharding import PartitionSpec as P

HEAD_DIM = 128
WORK = 128


def pack_pass(pairs, query_rows, key_rows, value_rows, out_grad, starts, proj_weight):
    row_count = query_rows.shape[0]
    head_count = proj_weight.shape[0] // HEAD_DIM
    root_dim = math.sqrt(HEAD_DIM)
    used = jnp.sum((starts >= 0).astype(jnp.int32))
    place = lax.broadcasted_iota(jnp.int32, (WORK, 1), 0)
    own_place = (used > WORK) | (place < used)
    flip = (
        lax.broadcasted_iota(jnp.int32, (WORK, WORK), 0)
        + lax.broadcasted_iota(jnp.int32, (WORK, WORK), 1)
        == WORK - 1
    ).astype(jnp.bfloat16)

    def flipped(rows):
        return jnp.dot(flip, rows, preferred_element_type=jnp.float32).astype(jnp.bfloat16)

    def compact(rows):
        other = lax.ppermute(rows[WORK:], "dp", pairs)
        return jnp.where(own_place, rows[:WORK], flipped(other))

    def spread(work):
        other = flipped(lax.ppermute(work, "dp", pairs))
        rows = jnp.concatenate([work, other], axis=0)
        index = lax.broadcasted_iota(jnp.int32, (row_count, 1), 0)
        return jnp.where(index < used, rows, jnp.zeros_like(rows))

    grad_work = compact(out_grad)
    grad_all = lax.all_gather(grad_work, "mp", axis=1, tiled=True)
    query_heads = query_rows.reshape(row_count, head_count, HEAD_DIM)
    key_heads = key_rows.reshape(row_count, head_count, HEAD_DIM)
    value_heads = value_rows.reshape(row_count, head_count, HEAD_DIM)
    same_image = starts[:, None] == starts[None, :]
    valid_rows = (starts >= 0)[:, None]
    scores = (
        jnp.einsum("qhd,khd->hqk", query_heads, key_heads, preferred_element_type=jnp.float32)
        / root_dim
    )
    scores = jnp.where(same_image[None], scores, -jnp.inf)
    maxima = jnp.max(scores, axis=2, keepdims=True)
    weights = jnp.exp(scores - maxima)
    probabilities = weights / jnp.sum(weights, axis=2, keepdims=True)
    rounded = probabilities.astype(jnp.bfloat16)
    attended = jnp.einsum(
        "hqk,khd->qhd", rounded, value_heads, preferred_element_type=jnp.float32
    ).reshape(row_count, -1)
    attended = jnp.where(valid_rows, attended, 0.0).astype(jnp.bfloat16)
    attended_work = compact(attended)
    head_terms = jnp.dot(attended_work, proj_weight, preferred_element_type=jnp.float32)
    projected_work = lax.psum_scatter(
        head_terms.astype(jnp.bfloat16), "mp", scatter_dimension=1, tiled=True
    )
    projected = spread(projected_work)
    grad_attended_work = lax.dot_general(
        grad_all, proj_weight, (((1,), (1,)), ((), ())), preferred_element_type=jnp.float32
    ).astype(jnp.bfloat16)
    grad_attended = spread(grad_attended_work)
    grad_heads = grad_attended.reshape(row_count, head_count, HEAD_DIM)
    grad_value = jnp.einsum("hqk,qhd->khd", rounded, grad_heads, preferred_element_type=jnp.float32)
    grad_weights = jnp.einsum(
        "qhd,khd->hqk", grad_heads, value_heads, preferred_element_type=jnp.float32
    )
    correction = jnp.sum(probabilities * grad_weights, axis=2, keepdims=True)
    grad_scores = (probabilities * (grad_weights - correction) / root_dim).astype(jnp.bfloat16)
    grad_query = jnp.einsum(
        "hqk,khd->qhd", grad_scores, key_heads, preferred_element_type=jnp.float32
    )
    grad_key = jnp.einsum(
        "hqk,qhd->khd", grad_scores, query_heads, preferred_element_type=jnp.float32
    )

    def finish(gradient):
        return jnp.where(valid_rows, gradient.reshape(row_count, -1), 0.0).astype(jnp.bfloat16)

    return (projected, finish(grad_query), finish(grad_key), finish(grad_value))


def solution(mesh):
    packs = mesh.shape["dp"]
    pairs = [(i, (i + packs // 2) % packs) for i in range(packs)]

    def shards(query_rows, key_rows, value_rows, proj_weight, out_grad, image_starts):
        own = lax.dynamic_index_in_dim(image_starts, lax.axis_index("dp"), 0, keepdims=False)
        return pack_pass(pairs, query_rows, key_rows, value_rows, out_grad, own, proj_weight)

    placed = (P("dp", "mp"), P("dp", "mp"), P("dp", "mp"), P("mp", None), P("dp", "mp"), P())
    return jax.shard_map(
        shards,
        mesh=mesh,
        in_specs=placed,
        out_specs=(P("dp", "mp"), P("dp", "mp"), P("dp", "mp"), P("dp", "mp")),
        check_vma=False,
    )
```

```python
import functools
import math

import jax
import jax.numpy as jnp
from jax import lax
from jax.experimental import pallas as pl
from jax.experimental.pallas import tpu as pltpu
from jax.sharding import PartitionSpec as P

HEAD_DIM = 128
WORK = 128
PIECE = 384
PIECE_HEADS = PIECE // HEAD_DIM
ROOT = math.sqrt(HEAD_DIM)
F32 = jnp.float32
BF16 = jnp.bfloat16
NT = (((1,), (1,)), ((), ()))
TN = (((0,), (0,)), ((), ()))


def kernel(packs, groups, q_ref, k_ref, v_ref, og_ref, row_ref, col_ref, w_hbm,
           proj_ref, gq_ref, gk_ref, gv_ref,
           w_buf, prob, att_lo, att_hi, att_in, att_work, og_in, gath, ga_acc,
           ga_lo, ga_out, ga_in, rs_in, rs_out, pr_work, pr_in,
           w_sem, og_send, og_recv, att_send, att_recv, ga_send, ga_recv, pr_send, pr_recv,
           up_send, down_send, ag_recv, rs_send, rs_recv):
    sub = q_ref.shape[1] // PIECE
    total = groups * sub
    z = lax.axis_index("mp")
    dp = lax.axis_index("dp")
    partner = lax.rem(dp + packs // 2, packs)
    has_low = z > 0
    has_high = z < groups - 1

    def remote(src, dst, send, recv, where):
        return pltpu.make_async_remote_copy(
            src_ref=src, dst_ref=dst, send_sem=send, recv_sem=recv,
            device_id=where, device_id_type=pl.DeviceIdType.MESH,
        )

    pair = {"dp": partner}
    high = {"mp": lax.rem(z + 1, groups)}
    low = {"mp": lax.rem(z + groups - 1, groups)}

    barrier = pltpu.get_barrier_semaphore()
    pl.semaphore_signal(barrier, inc=1, device_id=pair, device_id_type=pl.DeviceIdType.MESH)

    @pl.when(has_low)
    def _():
        pl.semaphore_signal(barrier, inc=1, device_id=low, device_id_type=pl.DeviceIdType.MESH)

    @pl.when(has_high)
    def _():
        pl.semaphore_signal(barrier, inc=1, device_id=high, device_id_type=pl.DeviceIdType.MESH)

    def w_copy(p):
        columns = pl.ds(pl.multiple_of(p * PIECE, PIECE), PIECE)
        return pltpu.make_async_copy(w_hbm.at[:, columns], w_buf.at[p], w_sem.at[p])

    @pl.loop(0, total)
    def _(j):
        w_copy(lax.rem(z * sub + j, total)).start()

    pl.semaphore_wait(
        barrier, 1 + has_low.astype(jnp.int32) + has_high.astype(jnp.int32)
    )

    def cols(k):
        return slice(k * PIECE, (k + 1) * PIECE)

    def og_copy(k):
        return remote(og_ref.at[pl.ds(WORK, WORK), pl.ds(k * PIECE, PIECE)], og_in.at[k],
                      og_send.at[k], og_recv.at[k], pair)

    def att_copy(k):
        return remote(att_hi.at[k], att_in.at[k], att_send.at[k], att_recv.at[k], pair)

    def ga_copy(k):
        return remote(ga_out.at[k], ga_in.at[k], ga_send.at[k], ga_recv.at[k], pair)

    def pr_copy(k):
        return remote(pr_work.at[k], pr_in.at[k], pr_send.at[k], pr_recv.at[k], pair)

    early = (sub + 1) // 2
    for k in range(early):
        og_copy(k).start()

    starts_row = row_ref[...]
    used = jnp.sum((starts_row >= 0).astype(jnp.int32), axis=1, keepdims=True)
    place = lax.broadcasted_iota(jnp.int32, (WORK, PIECE), 0)
    own_place = (used > WORK) | (place < used)
    valid_lo = place < used
    valid_hi = place + WORK < used
    square = (WORK, WORK)
    flip = (
        lax.broadcasted_iota(jnp.int32, square, 0) + lax.broadcasted_iota(jnp.int32, square, 1)
        == WORK - 1
    ).astype(BF16)

    def flipped(rows):
        return jnp.dot(flip, rows, preferred_element_type=F32)

    def keep(mask, rows):
        return jnp.where(mask, rows, 0.0).astype(BF16)

    def forward(k):
        for s in range(2):
            rows = slice(s * WORK, (s + 1) * WORK)
            same = col_ref[rows, :] == row_ref[:, rows]
            parts = []
            for j in range(PIECE_HEADS):
                h = k * PIECE_HEADS + j
                c = slice(h * HEAD_DIM, (h + 1) * HEAD_DIM)
                score = lax.dot_general(q_ref[rows, c], k_ref[rows, c], NT,
                                        preferred_element_type=F32) / ROOT
                score = jnp.where(same, score, -1e30)
                weight = jnp.exp(score - jnp.max(score, axis=1, keepdims=True))
                chance = weight / jnp.sum(weight, axis=1, keepdims=True)
                prob[2 * h + s] = chance
                parts.append(jnp.dot(chance.astype(BF16), v_ref[rows, c],
                                     preferred_element_type=F32))
            parts = jnp.concatenate(parts, axis=1)
            if s == 0:
                att_lo[k] = keep(valid_lo, parts)
            else:
                att_hi[k] = keep(valid_hi, parts)
        att_copy(k).start()

    def send_own(k):
        og_copy(k).wait_recv()
        p = z * sub + k
        gath[p] = jnp.where(own_place, og_ref[0:WORK, cols(k)].astype(F32),
                            flipped(og_in[k])).astype(BF16)

        @pl.when(has_high)
        def _():
            ag_up(p).start()

        @pl.when(has_low)
        def _():
            ag_down(p).start()

    def ag_up(p):
        return remote(gath.at[p], gath.at[p], up_send.at[p], ag_recv.at[p], high)

    def ag_down(p):
        return remote(gath.at[p], gath.at[p], down_send.at[p], ag_recv.at[p], low)

    def ga_add(p):
        ga_acc[...] += lax.dot_general(gath[p], w_buf[p], NT, preferred_element_type=F32)

    def gather_item(i):
        d, k = i // sub, lax.rem(i, sub)
        below, above = z - d, z + d

        @pl.when(below >= 0)
        def _():
            p = below * sub + k
            ag_up(p).wait_recv()

            @pl.when(has_high)
            def _():
                ag_up(p).start()

        @pl.when(above < groups)
        def _():
            p = above * sub + k
            ag_down(p).wait_recv()

            @pl.when(has_low)
            def _():
                ag_down(p).start()

    def gather_add(i):
        d, k = i // sub, lax.rem(i, sub)
        below, above = z - d, z + d

        @pl.when(below >= 0)
        def _():
            ga_add(below * sub + k)

        @pl.when(above < groups)
        def _():
            ga_add(above * sub + k)

    def partial(p):
        result = jnp.dot(att_work[:, 0:PIECE], w_buf[p, 0:PIECE, :], preferred_element_type=F32)
        for k in range(1, sub):
            result += jnp.dot(att_work[:, cols(k)], w_buf[p, cols(k), :],
                              preferred_element_type=F32)
        return result

    def rs_up(p):
        return remote(rs_out.at[p], rs_in.at[p], rs_send.at[p], rs_recv.at[p], high)

    def rs_down(p, slot):
        return remote(rs_out.at[p], rs_in.at[slot], rs_send.at[p], rs_recv.at[slot], low)

    def scatter_slot(n):
        i = n - z
        c, k = groups - 1 - i // sub, lax.rem(i, sub)

        @pl.when((i >= 0) & (c > z))
        def _():
            p = c * sub + k
            result = partial(p)

            @pl.when(has_low)
            def _():
                rs_up(p).wait_recv()
                rs_out[p] = (result + rs_in[p].astype(F32)).astype(BF16)

            @pl.when(jnp.logical_not(has_low))
            def _():
                rs_out[p] = result.astype(BF16)

            rs_up(p).start()

        i2 = n - (groups - 1 - z)
        c2, k2 = i2 // sub, lax.rem(i2, sub)

        @pl.when((i2 >= 0) & (c2 < z))
        def _():
            p = c2 * sub + k2
            result = partial(p)

            @pl.when(has_high)
            def _():
                rs_down(p, p).wait_recv()
                rs_out[p] = (result + rs_in[p].astype(F32)).astype(BF16)

            @pl.when(jnp.logical_not(has_high))
            def _():
                rs_out[p] = result.astype(BF16)

            slot = jnp.where(c2 == z - 1, total + k2, p)
            rs_down(p, slot).start()

    def scatter_end(k):
        p = z * sub + k
        ga_acc[:, 0:PIECE] = partial(p)

        @pl.when(has_low)
        def _():
            rs_up(p).wait_recv()
            ga_acc[:, 0:PIECE] += rs_in[p].astype(F32)

        @pl.when(has_high)
        def _():
            rs_down(p, total + k).wait_recv()
            ga_acc[:, 0:PIECE] += rs_in[total + k].astype(F32)

        pr_work[k] = ga_acc[:, 0:PIECE].astype(BF16)
        pr_copy(k).start()

    def backward(k, s, grads):
        rows = slice(s * WORK, (s + 1) * WORK)
        valid = (valid_lo if s == 0 else valid_hi)[:, 0:HEAD_DIM]
        for j in range(PIECE_HEADS):
            h = k * PIECE_HEADS + j
            c = slice(h * HEAD_DIM, (h + 1) * HEAD_DIM)
            chance = prob[2 * h + s]
            grad = grads[:, j * HEAD_DIM:(j + 1) * HEAD_DIM]
            gv = lax.dot_general(chance.astype(BF16), grad, TN, preferred_element_type=F32)
            gw = lax.dot_general(grad, v_ref[rows, c], NT, preferred_element_type=F32)
            correction = jnp.sum(chance * gw, axis=1, keepdims=True)
            gs = (chance * (gw - correction) / ROOT).astype(BF16)
            gq = jnp.dot(gs, k_ref[rows, c], preferred_element_type=F32)
            gk = lax.dot_general(gs, q_ref[rows, c], TN, preferred_element_type=F32)
            gv_ref[rows, c] = keep(valid, gv)
            gq_ref[rows, c] = keep(valid, gq)
            gk_ref[rows, c] = keep(valid, gk)

    sent = 0
    for k in range(sub):
        forward(k)
        if k % 2 == 1 and sent < early:
            send_own(sent)
            sent += 1
    for k in range(early, sub):
        og_copy(k).start()
    for k in range(sent, early):
        send_own(k)
    ga_acc[...] = jnp.zeros_like(ga_acc)

    @pl.loop(0, total)
    def _(j):
        w_copy(j).wait()

    for k in range(early):
        ga_add(z * sub + k)
    steps = (groups - 1) * sub
    slots = steps + groups - 1
    if groups > 1:
        for k in range(early):
            gather_item(jnp.int32(sub + k))

    for k in range(sub):
        att_copy(k).wait_recv()
        att_work[:, cols(k)] = jnp.where(own_place, att_lo[k].astype(F32),
                                         flipped(att_in[k])).astype(BF16)

    done = 0
    for k in range(early, sub):
        scatter_slot(jnp.int32(done))
        done += 1
        send_own(k)
    for k in range(early):
        gather_add(jnp.int32(sub + k))

    @pl.loop(0, steps - early)
    def _(n):
        gather_item(n + sub + early)
        scatter_slot(n + done)
        gather_add(n + sub + early)

    for k in range(early, sub):
        ga_add(z * sub + k)
    done += steps - early

    for k in range(sub):
        piece = ga_acc[:, cols(k)].astype(BF16)
        ga_out[k] = piece
        ga_lo[k] = jnp.where(valid_lo, piece.astype(F32), 0.0).astype(BF16)
        ga_copy(k).start()

    @pl.loop(done, slots)
    def _(n):
        scatter_slot(n)

    for k in range(sub):
        scatter_end(k)
        backward(k, 0, ga_lo[k])

    for k in range(sub):
        ga_copy(k).wait_recv()
        backward(k, 1, keep(valid_hi, flipped(ga_in[k])))

    for k in range(sub):
        pr_copy(k).wait_recv()
        proj_ref[0:WORK, cols(k)] = keep(valid_lo, pr_work[k].astype(F32))
        proj_ref[WORK:2 * WORK, cols(k)] = keep(valid_hi, flipped(pr_in[k]))

    for k in range(sub):
        og_copy(k).wait_send()
        att_copy(k).wait_send()
        ga_copy(k).wait_send()
        pr_copy(k).wait_send()

    @pl.loop(0, total)
    def _(p):
        c = p // sub

        @pl.when(has_high & (c <= z))
        def _():
            ag_up(p).wait_send()

        @pl.when(has_low & (c >= z))
        def _():
            ag_down(p).wait_send()

        @pl.when(c != z)
        def _():
            rs_up(p).wait_send()


def solution(mesh):
    packs, groups = mesh.shape["dp"], mesh.shape["mp"]

    def shards(query_rows, key_rows, value_rows, proj_weight, out_grad, image_starts):
        rows, width = query_rows.shape
        sub = width // PIECE
        total = groups * sub
        own = lax.dynamic_index_in_dim(image_starts, lax.axis_index("dp"), 0, keepdims=False)
        across = own[None, :]
        down = jnp.broadcast_to(own[:, None], (rows, WORK))
        vmem = pl.BlockSpec(memory_space=pltpu.VMEM)
        dma = pltpu.SemaphoreType.DMA
        block = jax.ShapeDtypeStruct((rows, width), BF16)

        def pieces(count):
            return pltpu.VMEM((count, WORK, PIECE), BF16)

        return pl.pallas_call(
            functools.partial(kernel, packs, groups),
            out_shape=(block,) * 4,
            in_specs=[vmem] * 6 + [pl.BlockSpec(memory_space=pl.ANY)],
            out_specs=(vmem,) * 4,
            scratch_shapes=[
                pltpu.VMEM((total, width, PIECE), BF16),
                pltpu.VMEM((2 * width // HEAD_DIM, WORK, WORK), F32),
                pieces(sub), pieces(sub), pieces(sub),
                pltpu.VMEM((WORK, width), BF16),
                pieces(sub), pieces(total),
                pltpu.VMEM((WORK, width), F32),
                pieces(sub), pieces(sub), pieces(sub),
                pieces(total + sub), pieces(total),
                pieces(sub), pieces(sub),
                dma((total,)),
                dma((sub,)), dma((sub,)), dma((sub,)), dma((sub,)),
                dma((sub,)), dma((sub,)), dma((sub,)), dma((sub,)),
                dma((total,)), dma((total,)), dma((total,)),
                dma((total,)), dma((total + sub,)),
            ],
            compiler_params=pltpu.CompilerParams(
                collective_id=0, has_side_effects=True, vmem_limit_bytes=60 * 2**20
            ),
            cost_estimate=pl.CostEstimate(
                flops=4 * WORK * width * width * groups,
                bytes_accessed=2 * width * width * groups + 16 * rows * width,
                transcendentals=rows * width,
            ),
        )(query_rows, key_rows, value_rows, out_grad, across, down, proj_weight)

    placed = (P("dp", "mp"), P("dp", "mp"), P("dp", "mp"), P("mp", None), P("dp", "mp"), P())
    return jax.shard_map(
        shards,
        mesh=mesh,
        in_specs=placed,
        out_specs=(P("dp", "mp"), P("dp", "mp"), P("dp", "mp"), P("dp", "mp")),
        check_vma=False,
    )
```

```python
import functools
import math

import jax
import jax.numpy as jnp
from jax import lax
from jax.experimental import pallas as pl
from jax.experimental.pallas import tpu as pltpu
from jax.sharding import PartitionSpec as P

HEAD_DIM = 128
WORK = 128
ROOT = math.sqrt(HEAD_DIM)
F32 = jnp.float32
BF16 = jnp.bfloat16
NT = (((1,), (1,)), ((), ()))
TN = (((0,), (0,)), ((), ()))


def piece_width(width):
    return 512 if width % 512 == 0 else 384


def kernel(packs, groups, q_hbm, k_hbm, v_hbm, og_hbm, starts_ref, w_hbm,
           proj_out, gq_out, gk_out, gv_out,
           q_ref, k_ref, v_ref, og_ref, proj_ref, gq_ref, gk_ref, gv_ref,
           bias, w_buf, prob, att_lo, att_hi, att_in, att_work, og_in, gath, ga_acc, pr_acc,
           ga_lo, ga_out, ga_in, rs_in, rs_out, pr_work, pr_in,
           in_sem, out_sem, w_sem, og_send, og_recv, att_send, att_recv,
           ga_send, ga_recv, pr_send, pr_recv, up_send, down_send, ag_recv, rs_send, rs_recv):
    width = q_ref.shape[1]
    PIECE = piece_width(width)
    PIECE_HEADS = PIECE // HEAD_DIM
    sub = width // PIECE
    total = groups * sub
    z = lax.axis_index("mp")
    dp = lax.axis_index("dp")
    partner = lax.rem(dp + packs // 2, packs)
    has_low = z > 0
    has_high = z < groups - 1

    def remote(src, dst, send, recv, where):
        return pltpu.make_async_remote_copy(
            src_ref=src, dst_ref=dst, send_sem=send, recv_sem=recv,
            device_id=where, device_id_type=pl.DeviceIdType.MESH,
        )

    pair = {"dp": partner}
    high = {"mp": lax.rem(z + 1, groups)}
    low = {"mp": lax.rem(z + groups - 1, groups)}

    barrier = pltpu.get_barrier_semaphore()
    pl.semaphore_signal(barrier, inc=1, device_id=pair, device_id_type=pl.DeviceIdType.MESH)

    @pl.when(has_low)
    def _():
        pl.semaphore_signal(barrier, inc=1, device_id=low, device_id_type=pl.DeviceIdType.MESH)

    @pl.when(has_high)
    def _():
        pl.semaphore_signal(barrier, inc=1, device_id=high, device_id_type=pl.DeviceIdType.MESH)

    loads = [
        pltpu.make_async_copy(source, held, in_sem.at[n])
        for n, (source, held) in enumerate(
            [(og_hbm, og_ref), (q_hbm, q_ref), (k_hbm, k_ref), (v_hbm, v_ref)]
        )
    ]
    for load in loads:
        load.start()

    def w_copy(c):
        columns = pl.ds(pl.multiple_of(c * width, width), width)
        return pltpu.make_async_copy(w_hbm.at[:, columns], w_buf.at[c], w_sem.at[c])

    @pl.loop(0, groups)
    def _(j):
        w_copy(lax.rem(z + j, groups)).start()

    starts_row = starts_ref[pl.ds(dp, 1), :]
    for s in range(2):
        across = jnp.broadcast_to(
            starts_row[:, s * WORK:(s + 1) * WORK].astype(F32), (WORK, WORK)
        )
        bias[s] = jnp.where(across == across.T, 0.0, -1e30)

    pl.semaphore_wait(
        barrier, 1 + has_low.astype(jnp.int32) + has_high.astype(jnp.int32)
    )

    def cols(k):
        return slice(k * PIECE, (k + 1) * PIECE)

    def og_copy(k):
        return remote(og_hbm.at[pl.ds(WORK, WORK), pl.ds(k * PIECE, PIECE)], og_in.at[k],
                      og_send.at[k], og_recv.at[k], pair)

    def att_copy(k):
        return remote(att_hi.at[k], att_in.at[k], att_send.at[k], att_recv.at[k], pair)

    def ga_copy(k):
        return remote(ga_out.at[k], ga_in.at[k], ga_send.at[k], ga_recv.at[k], pair)

    def pr_copy(k):
        return remote(pr_work.at[k], pr_in.at[k], pr_send.at[k], pr_recv.at[k], pair)

    early = (sub + 1) // 2
    for k in range(early):
        og_copy(k).start()

    used = jnp.sum((starts_row >= 0).astype(jnp.int32), axis=1, keepdims=True)
    place = lax.broadcasted_iota(jnp.int32, (WORK, PIECE), 0)
    own_place = (used > WORK) | (place < used)
    valid_lo = place < used
    valid_hi = place + WORK < used
    square = (WORK, WORK)
    flip = (
        lax.broadcasted_iota(jnp.int32, square, 0) + lax.broadcasted_iota(jnp.int32, square, 1)
        == WORK - 1
    ).astype(BF16)

    def flipped(rows):
        return jnp.dot(flip, rows, preferred_element_type=F32)

    def keep(mask, rows):
        return jnp.where(mask, rows, 0.0).astype(BF16)

    def forward(k):
        for s in range(2):
            rows = slice(s * WORK, (s + 1) * WORK)
            mask = bias[s]
            parts = []
            for j in range(PIECE_HEADS):
                h = k * PIECE_HEADS + j
                c = slice(h * HEAD_DIM, (h + 1) * HEAD_DIM)
                score = lax.dot_general(q_ref[rows, c], k_ref[rows, c], NT,
                                        preferred_element_type=F32) * (1.0 / ROOT) + mask
                weight = jnp.exp(score - jnp.max(score, axis=1, keepdims=True))
                chance = weight * (1.0 / jnp.sum(weight, axis=1, keepdims=True))
                prob[2 * h + s] = chance
                parts.append(jnp.dot(chance.astype(BF16), v_ref[rows, c],
                                     preferred_element_type=F32))
            parts = jnp.concatenate(parts, axis=1)
            if s == 0:
                att_lo[k] = keep(valid_lo, parts)
            else:
                att_hi[k] = keep(valid_hi, parts)
        att_copy(k).start()

    def span(k):
        return pl.ds(pl.multiple_of(k * PIECE, PIECE), PIECE)

    def ag_up(s, k):
        block = gath.at[s, :, span(k)]
        p = s * sub + k
        return remote(block, block, up_send.at[p], ag_recv.at[p], high)

    def ag_down(s, k):
        block = gath.at[s, :, span(k)]
        p = s * sub + k
        return remote(block, block, down_send.at[p], ag_recv.at[p], low)

    def send_own(k):
        og_copy(k).wait_recv()
        gath[z, :, cols(k)] = jnp.where(own_place, og_ref[0:WORK, cols(k)].astype(F32),
                                        flipped(og_in[k])).astype(BF16)

        @pl.when(has_high)
        def _():
            ag_up(z, k).start()

        @pl.when(has_low)
        def _():
            ag_down(z, k).start()

    def shard_term(c):
        return lax.dot_general(gath[c], w_buf[c], NT, preferred_element_type=F32)

    def gather_item(i):
        d, k = i // sub, lax.rem(i, sub)
        below, above = z - d, z + d

        @pl.when(below >= 0)
        def _():
            ag_up(below, k).wait_recv()

            @pl.when(has_high)
            def _():
                ag_up(below, k).start()

        @pl.when(above < groups)
        def _():
            ag_down(above, k).wait_recv()

            @pl.when(has_low)
            def _():
                ag_down(above, k).start()

    farthest = jnp.maximum(z, groups - 1 - z)

    def gather_add(i):
        d, k = i // sub, lax.rem(i, sub)
        below, above = z - d, z + d

        @pl.when((below >= 0) & (k == sub - 1))
        def _():
            ga_acc[...] += shard_term(below)

        @pl.when((above < groups) & (k == sub - 1))
        def _():
            ga_acc[...] += shard_term(above)

        @pl.when((d == farthest) & (k == sub - 1))
        def _():
            for j in range(sub):
                piece = ga_acc[:, cols(j)].astype(BF16)
                ga_out[j] = piece
                ga_lo[j] = jnp.where(valid_lo, piece.astype(F32), 0.0).astype(BF16)
                ga_copy(j).start()

    def partial(c, k):
        return jnp.dot(att_work[...], w_buf[c, :, span(k)], preferred_element_type=F32)

    def rs_up(p):
        return remote(rs_out.at[p], rs_in.at[p], rs_send.at[p], rs_recv.at[p], high)

    def rs_down(p, slot):
        return remote(rs_out.at[p], rs_in.at[slot], rs_send.at[p], rs_recv.at[slot], low)

    up_end = jnp.where(has_low, (groups - 1 - z) * sub + z, 0)
    down_end = jnp.where(has_high, z * sub + groups - 1 - z, 0)
    end_slot = jnp.maximum(up_end, down_end)

    def scatter_slot(n):
        i = n - z
        c, k = groups - 1 - i // sub, lax.rem(i, sub)

        @pl.when((i >= 0) & (c > z))
        def _():
            p = c * sub + k
            result = partial(c, k)

            @pl.when(has_low)
            def _():
                rs_up(p).wait_recv()
                rs_out[p] = (result + rs_in[p].astype(F32)).astype(BF16)

            @pl.when(jnp.logical_not(has_low))
            def _():
                rs_out[p] = result.astype(BF16)

            rs_up(p).start()

        i2 = n - (groups - 1 - z)
        c2, k2 = i2 // sub, lax.rem(i2, sub)

        @pl.when((i2 >= 0) & (c2 < z))
        def _():
            p = c2 * sub + k2
            result = partial(c2, k2)

            @pl.when(has_high)
            def _():
                rs_down(p, p).wait_recv()
                rs_out[p] = (result + rs_in[p].astype(F32)).astype(BF16)

            @pl.when(jnp.logical_not(has_high))
            def _():
                rs_out[p] = result.astype(BF16)

            slot = jnp.where(c2 == z - 1, total + k2, p)
            rs_down(p, slot).start()

        k3 = n - end_slot

        @pl.when((k3 >= 0) & (k3 < sub))
        def _():
            scatter_end(k3)

    def scatter_end(k):
        p = z * sub + k
        pr_acc[...] = partial(z, k)

        @pl.when(has_low)
        def _():
            rs_up(p).wait_recv()
            pr_acc[...] += rs_in[p].astype(F32)

        @pl.when(has_high)
        def _():
            rs_down(p, total + k).wait_recv()
            pr_acc[...] += rs_in[total + k].astype(F32)

        pr_work[k] = pr_acc[...].astype(BF16)
        pr_copy(k).start()

    def backward(k, s, grads):
        rows = slice(s * WORK, (s + 1) * WORK)
        valid = (valid_lo if s == 0 else valid_hi)[:, 0:HEAD_DIM]
        for j in range(PIECE_HEADS):
            h = k * PIECE_HEADS + j
            c = slice(h * HEAD_DIM, (h + 1) * HEAD_DIM)
            chance = prob[2 * h + s]
            grad = grads[:, j * HEAD_DIM:(j + 1) * HEAD_DIM]
            gv = lax.dot_general(chance.astype(BF16), grad, TN, preferred_element_type=F32)
            gw = lax.dot_general(grad, v_ref[rows, c], NT, preferred_element_type=F32)
            correction = jnp.sum(chance * gw, axis=1, keepdims=True)
            gs = (chance * (gw - correction) * (1.0 / ROOT)).astype(BF16)
            gq = jnp.dot(gs, k_ref[rows, c], preferred_element_type=F32)
            gk = lax.dot_general(gs, q_ref[rows, c], TN, preferred_element_type=F32)
            gv_ref[rows, c] = keep(valid, gv)
            gq_ref[rows, c] = keep(valid, gq)
            gk_ref[rows, c] = keep(valid, gk)

    def results(s, first, last):
        rows = pl.ds(s * WORK, WORK)
        return [
            pltpu.make_async_copy(held.at[rows, :], target.at[rows, :], out_sem.at[2 * n + s])
            for n, (held, target) in enumerate(
                [(gq_ref, gq_out), (gk_ref, gk_out), (gv_ref, gv_out), (proj_ref, proj_out)]
            )
            if first <= n < last
        ]

    for load in loads:
        load.wait()
    sent = 0
    for k in range(sub):
        forward(k)
        if k % 2 == 1 and sent < early:
            send_own(sent)
            sent += 1
    for k in range(early, sub):
        og_copy(k).start()
    for k in range(sent, early):
        send_own(k)

    @pl.loop(0, groups)
    def _(c):
        w_copy(c).wait()

    steps = (groups - 1) * sub
    for k in range(early):
        gather_item(jnp.int32(sub + k))

    for k in range(sub):
        att_copy(k).wait_recv()
        att_work[:, cols(k)] = jnp.where(own_place, att_lo[k].astype(F32),
                                         flipped(att_in[k])).astype(BF16)

    done = sub - early
    for k in range(early, sub):
        scatter_slot(jnp.int32(k - early))
        send_own(k)
    ga_acc[...] = shard_term(z)
    for k in range(early):
        gather_add(jnp.int32(sub + k))

    @pl.loop(0, steps - early)
    def _(n):
        gather_item(n + sub + early)
        scatter_slot(n + done)
        gather_add(n + sub + early)

    @pl.loop(done + steps - early, steps + 1)
    def _(n):
        scatter_slot(n)

    for k in range(sub):
        backward(k, 0, ga_lo[k])
    for copy in results(0, 0, 3):
        copy.start()

    for k in range(sub):
        ga_copy(k).wait_recv()
        backward(k, 1, keep(valid_hi, flipped(ga_in[k])))
    for copy in results(1, 0, 3):
        copy.start()

    for k in range(sub):
        pr_copy(k).wait_recv()
        proj_ref[0:WORK, cols(k)] = keep(valid_lo, pr_work[k].astype(F32))
        proj_ref[WORK:2 * WORK, cols(k)] = keep(valid_hi, flipped(pr_in[k]))
    for s in range(2):
        results(s, 3, 4)[0].start()

    for k in range(sub):
        og_copy(k).wait_send()
        att_copy(k).wait_send()
        ga_copy(k).wait_send()
        pr_copy(k).wait_send()

    @pl.loop(0, total)
    def _(p):
        c, k = p // sub, lax.rem(p, sub)

        @pl.when(has_high & (c <= z))
        def _():
            ag_up(c, k).wait_send()

        @pl.when(has_low & (c >= z))
        def _():
            ag_down(c, k).wait_send()

        @pl.when(c != z)
        def _():
            rs_up(p).wait_send()

    for s in range(2):
        for copy in results(s, 0, 4):
            copy.wait()


def hand_over(a, b, c, d, out_a, out_b, out_c, out_d, sem):
    copies = [
        pltpu.make_async_copy(held, target, sem.at[n])
        for n, (held, target) in enumerate([(a, out_a), (b, out_b), (c, out_c), (d, out_d)])
    ]
    for copy in copies:
        copy.start()
    for copy in copies:
        copy.wait()


def solution(mesh):
    packs, groups = mesh.shape["dp"], mesh.shape["mp"]

    def shards(query_rows, key_rows, value_rows, proj_weight, out_grad, image_starts):
        rows, width = query_rows.shape
        piece = piece_width(width)
        sub = width // piece
        total = groups * sub
        vmem = pl.BlockSpec(memory_space=pltpu.VMEM)
        anywhere = pl.BlockSpec(memory_space=pl.ANY)
        dma = pltpu.SemaphoreType.DMA
        block = jax.ShapeDtypeStruct((rows, width), BF16)

        def pieces(count):
            return pltpu.VMEM((count, WORK, piece), BF16)

        results = pl.pallas_call(
            functools.partial(kernel, packs, groups),
            out_shape=(block,) * 4,
            in_specs=[anywhere] * 4 + [vmem, anywhere],
            out_specs=(anywhere,) * 4,
            scratch_shapes=[pltpu.VMEM((rows, width), BF16)] * 8 + [
                pltpu.VMEM((2, WORK, WORK), F32),
                pltpu.VMEM((groups, width, width), BF16),
                pltpu.VMEM((2 * width // HEAD_DIM, WORK, WORK), F32),
                pieces(sub), pieces(sub), pieces(sub),
                pltpu.VMEM((WORK, width), BF16),
                pieces(sub),
                pltpu.VMEM((groups, WORK, width), BF16),
                pltpu.VMEM((WORK, width), F32),
                pltpu.VMEM((WORK, piece), F32),
                pieces(sub), pieces(sub), pieces(sub),
                pieces(total + sub), pieces(total),
                pieces(sub), pieces(sub),
                dma((4,)), dma((8,)), dma((groups,)),
                dma((sub,)), dma((sub,)), dma((sub,)), dma((sub,)),
                dma((sub,)), dma((sub,)), dma((sub,)), dma((sub,)),
                dma((total,)), dma((total,)), dma((total,)),
                dma((total,)), dma((total + sub,)),
            ],
            compiler_params=pltpu.CompilerParams(
                collective_id=0, has_side_effects=True, vmem_limit_bytes=56 * 2**20
            ),
            cost_estimate=pl.CostEstimate(
                flops=4 * WORK * width * width * groups,
                bytes_accessed=2 * width * width * groups + 16 * rows * width,
                transcendentals=rows * width,
            ),
        )(query_rows, key_rows, value_rows, out_grad, image_starts, proj_weight)
        return pl.pallas_call(
            hand_over,
            out_shape=(block,) * 4,
            in_specs=[anywhere] * 4,
            out_specs=(anywhere,) * 4,
            scratch_shapes=[dma((4,))],
            compiler_params=pltpu.CompilerParams(vmem_limit_bytes=60 * 2**20),
        )(*results)

    placed = (P("dp", "mp"), P("dp", "mp"), P("dp", "mp"), P("mp", None), P("dp", "mp"), P())
    return jax.shard_map(
        shards,
        mesh=mesh,
        in_specs=placed,
        out_specs=(P("dp", "mp"), P("dp", "mp"), P("dp", "mp"), P("dp", "mp")),
        check_vma=False,
    )
```

```python
import functools
import math

import jax
import jax.numpy as jnp
from jax import lax
from jax.experimental import pallas as pl
from jax.experimental.pallas import tpu as pltpu
from jax.sharding import PartitionSpec as P

HEAD_DIM = 128
WORK = 128
ROOT = math.sqrt(HEAD_DIM)
F32 = jnp.float32
BF16 = jnp.bfloat16
NT = (((1,), (1,)), ((), ()))
TN = (((0,), (0,)), ((), ()))


def piece_width(width):
    return 512 if width % 512 == 0 else 384


def kernel(packs, groups, q_hbm, k_hbm, v_hbm, og_hbm, starts_ref, w_hbm,
           proj_out, gq_out, gk_out, gv_out,
           q_ref, k_ref, v_ref, og_ref, proj_ref, gq_ref, gk_ref, gv_ref,
           bias, w_buf, prob, att_lo, att_hi, att_in, att_work, og_in, gath, ga_acc, pr_acc,
           ga_lo, ga_out, ga_in, rs_in, rs_out, pr_work, pr_in,
           in_sem, out_sem, w_sem, og_send, og_recv, att_send, att_recv,
           ga_send, ga_recv, pr_send, pr_recv, up_send, down_send, ag_recv, rs_send, rs_recv):
    width = q_ref.shape[1]
    PIECE = piece_width(width)
    PIECE_HEADS = PIECE // HEAD_DIM
    sub = width // PIECE
    total = groups * sub
    z = lax.axis_index("mp")
    dp = lax.axis_index("dp")
    partner = lax.rem(dp + packs // 2, packs)
    has_low = z > 0
    has_high = z < groups - 1

    def remote(src, dst, send, recv, where):
        return pltpu.make_async_remote_copy(
            src_ref=src, dst_ref=dst, send_sem=send, recv_sem=recv,
            device_id=where, device_id_type=pl.DeviceIdType.MESH,
        )

    pair = {"dp": partner}
    high = {"mp": lax.rem(z + 1, groups)}
    low = {"mp": lax.rem(z + groups - 1, groups)}

    barrier = pltpu.get_barrier_semaphore()
    pl.semaphore_signal(barrier, inc=1, device_id=pair, device_id_type=pl.DeviceIdType.MESH)

    @pl.when(has_low)
    def _():
        pl.semaphore_signal(barrier, inc=1, device_id=low, device_id_type=pl.DeviceIdType.MESH)

    @pl.when(has_high)
    def _():
        pl.semaphore_signal(barrier, inc=1, device_id=high, device_id_type=pl.DeviceIdType.MESH)

    loads = [
        pltpu.make_async_copy(source, held, in_sem.at[n])
        for n, (source, held) in enumerate(
            [(og_hbm, og_ref), (q_hbm, q_ref), (k_hbm, k_ref), (v_hbm, v_ref)]
        )
    ]
    for load in loads:
        load.start()

    def w_copy(c):
        columns = pl.ds(pl.multiple_of(c * width, width), width)
        return pltpu.make_async_copy(w_hbm.at[:, columns], w_buf.at[c], w_sem.at[c])

    @pl.loop(0, groups)
    def _(j):
        w_copy(lax.rem(z + j, groups)).start()

    starts_row = starts_ref[pl.ds(dp, 1), :]
    for s in range(2):
        across = jnp.broadcast_to(
            starts_row[:, s * WORK:(s + 1) * WORK].astype(F32), (WORK, WORK)
        )
        bias[s] = jnp.where(across == across.T, 0.0, -1e30)

    pl.semaphore_wait(
        barrier, 1 + has_low.astype(jnp.int32) + has_high.astype(jnp.int32)
    )

    def cols(k):
        return slice(k * PIECE, (k + 1) * PIECE)

    def og_copy(k):
        return remote(og_hbm.at[pl.ds(WORK, WORK), pl.ds(k * PIECE, PIECE)], og_in.at[k],
                      og_send.at[k], og_recv.at[k], pair)

    def att_copy(k):
        return remote(att_hi.at[k], att_in.at[k], att_send.at[k], att_recv.at[k], pair)

    def ga_copy(k):
        return remote(ga_out.at[k], ga_in.at[k], ga_send.at[k], ga_recv.at[k], pair)

    def pr_copy(k):
        return remote(pr_work.at[k], pr_in.at[k], pr_send.at[k], pr_recv.at[k], pair)

    for k in range(sub):
        og_copy(k).start()

    used = jnp.sum((starts_row >= 0).astype(jnp.int32), axis=1, keepdims=True)
    place = lax.broadcasted_iota(jnp.int32, (WORK, PIECE), 0)
    own_place = (used > WORK) | (place < used)
    valid_lo = place < used
    valid_hi = place + WORK < used
    square = (WORK, WORK)
    flip = (
        lax.broadcasted_iota(jnp.int32, square, 0) + lax.broadcasted_iota(jnp.int32, square, 1)
        == WORK - 1
    ).astype(BF16)

    def flipped(rows):
        return jnp.dot(flip, rows, preferred_element_type=F32)

    def keep(mask, rows):
        return jnp.where(mask, rows, 0.0).astype(BF16)

    def forward(k):
        for s in range(2):
            rows = slice(s * WORK, (s + 1) * WORK)
            mask = bias[s]
            parts = []
            for j in range(PIECE_HEADS):
                h = k * PIECE_HEADS + j
                c = slice(h * HEAD_DIM, (h + 1) * HEAD_DIM)
                score = lax.dot_general(q_ref[rows, c], k_ref[rows, c], NT,
                                        preferred_element_type=F32) * (1.0 / ROOT) + mask
                weight = jnp.exp(score - jnp.max(score, axis=1, keepdims=True))
                chance = weight * (1.0 / jnp.sum(weight, axis=1, keepdims=True))
                prob[2 * h + s] = chance
                parts.append(jnp.dot(chance.astype(BF16), v_ref[rows, c],
                                     preferred_element_type=F32))
            parts = jnp.concatenate(parts, axis=1)
            if s == 0:
                att_lo[k] = keep(valid_lo, parts)
            else:
                att_hi[k] = keep(valid_hi, parts)
        att_copy(k).start()

    def span(k):
        return pl.ds(pl.multiple_of(k * PIECE, PIECE), PIECE)

    def ag_up(s, k):
        block = gath.at[s, :, span(k)]
        p = s * sub + k
        return remote(block, block, up_send.at[p], ag_recv.at[p], high)

    def ag_down(s, k):
        block = gath.at[s, :, span(k)]
        p = s * sub + k
        return remote(block, block, down_send.at[p], ag_recv.at[p], low)

    def send_own(k):
        og_copy(k).wait_recv()
        gath[z, :, cols(k)] = jnp.where(own_place, og_ref[0:WORK, cols(k)].astype(F32),
                                        flipped(og_in[k])).astype(BF16)

        @pl.when(has_high)
        def _():
            ag_up(z, k).start()

        @pl.when(has_low)
        def _():
            ag_down(z, k).start()

    def shard_term(c):
        return lax.dot_general(gath[c], w_buf[c], NT, preferred_element_type=F32)

    def gather_item(i):
        d, k = i // sub, lax.rem(i, sub)
        below, above = z - d, z + d

        @pl.when(below >= 0)
        def _():
            ag_up(below, k).wait_recv()

            @pl.when(has_high)
            def _():
                ag_up(below, k).start()

        @pl.when(above < groups)
        def _():
            ag_down(above, k).wait_recv()

            @pl.when(has_low)
            def _():
                ag_down(above, k).start()

    farthest = jnp.maximum(z, groups - 1 - z)

    def gather_add(i):
        d, k = i // sub, lax.rem(i, sub)
        below, above = z - d, z + d

        @pl.when((below >= 0) & (k == sub - 1))
        def _():
            ga_acc[...] += shard_term(below)

        @pl.when((above < groups) & (k == sub - 1))
        def _():
            ga_acc[...] += shard_term(above)

        @pl.when((d == farthest) & (k == sub - 1))
        def _():
            for j in range(sub):
                piece = ga_acc[:, cols(j)].astype(BF16)
                ga_out[j] = piece
                ga_lo[j] = jnp.where(valid_lo, piece.astype(F32), 0.0).astype(BF16)
                ga_copy(j).start()

    def partial(c, k):
        return jnp.dot(att_work[...], w_buf[c, :, span(k)], preferred_element_type=F32)

    def rs_up(p):
        return remote(rs_out.at[p], rs_in.at[p], rs_send.at[p], rs_recv.at[p], high)

    def rs_down(p, slot):
        return remote(rs_out.at[p], rs_in.at[slot], rs_send.at[p], rs_recv.at[slot], low)

    up_end = jnp.where(has_low, (groups - 1 - z) * sub + z, 0)
    down_end = jnp.where(has_high, z * sub + groups - 1 - z, 0)
    end_slot = jnp.maximum(up_end, down_end)

    def scatter_slot(n):
        i = n - z
        c, k = groups - 1 - i // sub, lax.rem(i, sub)

        @pl.when((i >= 0) & (c > z))
        def _():
            p = c * sub + k
            result = partial(c, k)

            @pl.when(has_low)
            def _():
                rs_up(p).wait_recv()
                rs_out[p] = (result + rs_in[p].astype(F32)).astype(BF16)

            @pl.when(jnp.logical_not(has_low))
            def _():
                rs_out[p] = result.astype(BF16)

            rs_up(p).start()

        i2 = n - (groups - 1 - z)
        c2, k2 = i2 // sub, lax.rem(i2, sub)

        @pl.when((i2 >= 0) & (c2 < z))
        def _():
            p = c2 * sub + k2
            result = partial(c2, k2)

            @pl.when(has_high)
            def _():
                rs_down(p, p).wait_recv()
                rs_out[p] = (result + rs_in[p].astype(F32)).astype(BF16)

            @pl.when(jnp.logical_not(has_high))
            def _():
                rs_out[p] = result.astype(BF16)

            slot = jnp.where(c2 == z - 1, total + k2, p)
            rs_down(p, slot).start()

        k3 = n - end_slot

        @pl.when((k3 >= 0) & (k3 < sub))
        def _():
            scatter_end(k3)

    def scatter_end(k):
        p = z * sub + k
        pr_acc[...] = partial(z, k)

        @pl.when(has_low)
        def _():
            rs_up(p).wait_recv()
            pr_acc[...] += rs_in[p].astype(F32)

        @pl.when(has_high)
        def _():
            rs_down(p, total + k).wait_recv()
            pr_acc[...] += rs_in[total + k].astype(F32)

        pr_work[k] = pr_acc[...].astype(BF16)
        pr_copy(k).start()

    def backward(k, s, grads):
        rows = slice(s * WORK, (s + 1) * WORK)
        valid = (valid_lo if s == 0 else valid_hi)[:, 0:HEAD_DIM]
        for j in range(PIECE_HEADS):
            h = k * PIECE_HEADS + j
            c = pl.ds(pl.multiple_of(h * HEAD_DIM, HEAD_DIM), HEAD_DIM)
            chance = prob[2 * h + s]
            grad = grads[:, j * HEAD_DIM:(j + 1) * HEAD_DIM]
            gv = lax.dot_general(chance.astype(BF16), grad, TN, preferred_element_type=F32)
            gw = lax.dot_general(grad, v_ref[rows, c], NT, preferred_element_type=F32)
            correction = jnp.sum(chance * gw, axis=1, keepdims=True)
            gs = (chance * (gw - correction) * (1.0 / ROOT)).astype(BF16)
            gq = jnp.dot(gs, k_ref[rows, c], preferred_element_type=F32)
            gk = lax.dot_general(gs, q_ref[rows, c], TN, preferred_element_type=F32)
            gv_ref[rows, c] = keep(valid, gv)
            gq_ref[rows, c] = keep(valid, gq)
            gk_ref[rows, c] = keep(valid, gk)

    def results(s, first, last):
        rows = pl.ds(s * WORK, WORK)
        return [
            pltpu.make_async_copy(held.at[rows, :], target.at[rows, :], out_sem.at[2 * n + s])
            for n, (held, target) in enumerate(
                [(gq_ref, gq_out), (gk_ref, gk_out), (gv_ref, gv_out), (proj_ref, proj_out)]
            )
            if first <= n < last
        ]

    for load in loads:
        load.wait()
    for k in range(sub):
        forward(k)
        send_own(k)
    for k in range(sub):
        gather_item(jnp.int32(sub + k))

    @pl.loop(0, groups)
    def _(c):
        w_copy(c).wait()

    ga_acc[...] = shard_term(z)
    gather_add(jnp.int32(2 * sub - 1))

    steps = (groups - 1) * sub
    for k in range(sub):
        att_copy(k).wait_recv()
        att_work[:, cols(k)] = jnp.where(own_place, att_lo[k].astype(F32),
                                         flipped(att_in[k])).astype(BF16)
        if k < sub - 1:
            gather_item(jnp.int32(2 * sub + k))
    scatter_slot(jnp.int32(0))
    gather_item(jnp.int32(3 * sub - 1))
    scatter_slot(jnp.int32(1))
    gather_add(jnp.int32(3 * sub - 1))
    ahead = 2

    @pl.loop(0, steps - 2 * sub)
    def _(n):
        scatter_slot(n + ahead)
        gather_item(n + 3 * sub)
        gather_add(n + 3 * sub)

    ahead += steps - 2 * sub

    @pl.loop(0, sub)
    def _(k):
        scatter_slot(k + ahead)
        backward(k, 0, ga_lo[k])

    ahead += sub
    for copy in results(0, 0, 3):
        copy.start()

    @pl.loop(0, sub)
    def _(k):
        @pl.when(k < sub - 1)
        def _():
            scatter_slot(k + ahead)

        ga_copy(k).wait_recv()
        backward(k, 1, keep(valid_hi, flipped(ga_in[k])))

    for copy in results(1, 0, 3):
        copy.start()

    for k in range(sub):
        pr_copy(k).wait_recv()
        proj_ref[0:WORK, cols(k)] = keep(valid_lo, pr_work[k].astype(F32))
        proj_ref[WORK:2 * WORK, cols(k)] = keep(valid_hi, flipped(pr_in[k]))
    for s in range(2):
        results(s, 3, 4)[0].start()

    for k in range(sub):
        og_copy(k).wait_send()
        att_copy(k).wait_send()
        ga_copy(k).wait_send()
        pr_copy(k).wait_send()

    @pl.loop(0, total)
    def _(p):
        c, k = p // sub, lax.rem(p, sub)

        @pl.when(has_high & (c <= z))
        def _():
            ag_up(c, k).wait_send()

        @pl.when(has_low & (c >= z))
        def _():
            ag_down(c, k).wait_send()

        @pl.when(c != z)
        def _():
            rs_up(p).wait_send()

    for s in range(2):
        for copy in results(s, 0, 4):
            copy.wait()


def hand_over(*refs):
    sources, targets, (held, in_sem, out_sem) = refs[:4], refs[4:8], refs[8:]
    half = sources[0].shape[0] // 2
    loads, stores = [], []
    for s in range(2):
        rows = pl.ds(s * half, half)
        for n in range(4):
            spot = held.at[n, rows, :]
            loads.append(pltpu.make_async_copy(sources[n].at[rows, :], spot, in_sem.at[n, s]))
            stores.append(pltpu.make_async_copy(spot, targets[n].at[rows, :], out_sem.at[n, s]))
    for load in loads:
        load.start()
    for load, store in zip(loads, stores):
        load.wait()
        store.start()
    for store in stores:
        store.wait()


def solution(mesh):
    packs, groups = mesh.shape["dp"], mesh.shape["mp"]

    def shards(query_rows, key_rows, value_rows, proj_weight, out_grad, image_starts):
        rows, width = query_rows.shape
        piece = piece_width(width)
        sub = width // piece
        total = groups * sub
        vmem = pl.BlockSpec(memory_space=pltpu.VMEM)
        anywhere = pl.BlockSpec(memory_space=pl.ANY)
        dma = pltpu.SemaphoreType.DMA
        block = jax.ShapeDtypeStruct((rows, width), BF16)

        def pieces(count):
            return pltpu.VMEM((count, WORK, piece), BF16)

        results = pl.pallas_call(
            functools.partial(kernel, packs, groups),
            out_shape=(block,) * 4,
            in_specs=[anywhere] * 4 + [vmem, anywhere],
            out_specs=(anywhere,) * 4,
            scratch_shapes=[pltpu.VMEM((rows, width), BF16)] * 8 + [
                pltpu.VMEM((2, WORK, WORK), F32),
                pltpu.VMEM((groups, width, width), BF16),
                pltpu.VMEM((2 * width // HEAD_DIM, WORK, WORK), F32),
                pieces(sub), pieces(sub), pieces(sub),
                pltpu.VMEM((WORK, width), BF16),
                pieces(sub),
                pltpu.VMEM((groups, WORK, width), BF16),
                pltpu.VMEM((WORK, width), F32),
                pltpu.VMEM((WORK, piece), F32),
                pieces(sub), pieces(sub), pieces(sub),
                pieces(total + sub), pieces(total),
                pieces(sub), pieces(sub),
                dma((4,)), dma((8,)), dma((groups,)),
                dma((sub,)), dma((sub,)), dma((sub,)), dma((sub,)),
                dma((sub,)), dma((sub,)), dma((sub,)), dma((sub,)),
                dma((total,)), dma((total,)), dma((total,)),
                dma((total,)), dma((total + sub,)),
            ],
            compiler_params=pltpu.CompilerParams(
                collective_id=0, has_side_effects=True, vmem_limit_bytes=56 * 2**20
            ),
            cost_estimate=pl.CostEstimate(
                flops=4 * WORK * width * width * groups,
                bytes_accessed=2 * width * width * groups + 16 * rows * width,
                transcendentals=rows * width,
            ),
        )(query_rows, key_rows, value_rows, out_grad, image_starts, proj_weight)
        return pl.pallas_call(
            hand_over,
            out_shape=(block,) * 4,
            in_specs=[anywhere] * 4,
            out_specs=(anywhere,) * 4,
            scratch_shapes=[pltpu.VMEM((4, rows, width), BF16), dma((4, 2)), dma((4, 2))],
            compiler_params=pltpu.CompilerParams(vmem_limit_bytes=60 * 2**20),
        )(*results)

    placed = (P("dp", "mp"), P("dp", "mp"), P("dp", "mp"), P("mp", None), P("dp", "mp"), P())
    return jax.shard_map(
        shards,
        mesh=mesh,
        in_specs=placed,
        out_specs=(P("dp", "mp"), P("dp", "mp"), P("dp", "mp"), P("dp", "mp")),
        check_vma=False,
    )
```

```python
import functools
import math

import jax
import jax.numpy as jnp
from jax import lax
from jax.experimental import pallas as pl
from jax.experimental.pallas import tpu as pltpu
from jax.sharding import PartitionSpec as P

HEAD_DIM = 128
WORK = 128
ROOT = math.sqrt(HEAD_DIM)
F32 = jnp.float32
BF16 = jnp.bfloat16
NT = (((1,), (1,)), ((), ()))
TN = (((0,), (0,)), ((), ()))


def piece_width(width):
    return 512 if width % 512 == 0 else 384


def kernel(packs, groups, q_hbm, k_hbm, v_hbm, og_hbm, starts_ref, w_hbm,
           proj_out, gq_out, gk_out, gv_out,
           q_ref, k_ref, v_ref, og_ref, proj_ref, gq_ref, gk_ref, gv_ref,
           bias, w_buf, prob, att_lo, att_hi, att_in, att_work, og_in, gath, ga_acc, pr_acc,
           ga_lo, ga_out, ga_in, rs_in, rs_out, pr_work, pr_in,
           in_sem, out_sem, w_sem, og_send, og_recv, att_send, att_recv,
           ga_send, ga_recv, pr_send, pr_recv, up_send, down_send, ag_recv, rs_send, rs_recv):
    width = q_ref.shape[1]
    PIECE = piece_width(width)
    PIECE_HEADS = PIECE // HEAD_DIM
    sub = width // PIECE
    total = groups * sub
    z = lax.axis_index("mp")
    dp = lax.axis_index("dp")
    partner = lax.rem(dp + packs // 2, packs)
    has_low = z > 0
    has_high = z < groups - 1

    def remote(src, dst, send, recv, where):
        return pltpu.make_async_remote_copy(
            src_ref=src, dst_ref=dst, send_sem=send, recv_sem=recv,
            device_id=where, device_id_type=pl.DeviceIdType.MESH,
        )

    pair = {"dp": partner}
    high = {"mp": lax.rem(z + 1, groups)}
    low = {"mp": lax.rem(z + groups - 1, groups)}

    barrier = pltpu.get_barrier_semaphore()
    pl.semaphore_signal(barrier, inc=1, device_id=pair, device_id_type=pl.DeviceIdType.MESH)

    @pl.when(has_low)
    def _():
        pl.semaphore_signal(barrier, inc=1, device_id=low, device_id_type=pl.DeviceIdType.MESH)

    @pl.when(has_high)
    def _():
        pl.semaphore_signal(barrier, inc=1, device_id=high, device_id_type=pl.DeviceIdType.MESH)

    loads = [
        pltpu.make_async_copy(source, held, in_sem.at[n])
        for n, (source, held) in enumerate(
            [(og_hbm, og_ref), (q_hbm, q_ref), (k_hbm, k_ref), (v_hbm, v_ref)]
        )
    ]
    for load in loads:
        load.start()

    def w_copy(c):
        columns = pl.ds(pl.multiple_of(c * width, width), width)
        return pltpu.make_async_copy(w_hbm.at[:, columns], w_buf.at[c], w_sem.at[c])

    @pl.loop(0, groups)
    def _(j):
        w_copy(lax.rem(z + j, groups)).start()

    starts_row = starts_ref[pl.ds(dp, 1), :]
    for s in range(2):
        across = jnp.broadcast_to(
            starts_row[:, s * WORK:(s + 1) * WORK].astype(F32), (WORK, WORK)
        )
        bias[s] = jnp.where(across == across.T, 0.0, -1e30)

    pl.semaphore_wait(
        barrier, 1 + has_low.astype(jnp.int32) + has_high.astype(jnp.int32)
    )

    def cols(k):
        return slice(k * PIECE, (k + 1) * PIECE)

    def og_copy(k):
        return remote(og_hbm.at[pl.ds(WORK, WORK), pl.ds(k * PIECE, PIECE)], og_in.at[k],
                      og_send.at[k], og_recv.at[k], pair)

    def att_copy(k):
        return remote(att_hi.at[k], att_in.at[k], att_send.at[k], att_recv.at[k], pair)

    def ga_copy(k):
        return remote(ga_out.at[k], ga_in.at[k], ga_send.at[k], ga_recv.at[k], pair)

    def pr_copy(k):
        return remote(pr_work.at[k], pr_in.at[k], pr_send.at[k], pr_recv.at[k], pair)

    early = max(1, sub - 1)
    og_copy(0).start()

    used = jnp.sum((starts_row >= 0).astype(jnp.int32), axis=1, keepdims=True)
    place = lax.broadcasted_iota(jnp.int32, (WORK, PIECE), 0)
    own_place = (used > WORK) | (place < used)
    valid_lo = place < used
    valid_hi = place + WORK < used
    square = (WORK, WORK)
    flip = (
        lax.broadcasted_iota(jnp.int32, square, 0) + lax.broadcasted_iota(jnp.int32, square, 1)
        == WORK - 1
    ).astype(BF16)

    def flipped(rows):
        return jnp.dot(flip, rows, preferred_element_type=F32)

    def keep(mask, rows):
        return jnp.where(mask, rows, 0.0).astype(BF16)

    def forward(k):
        for s in range(2):
            rows = slice(s * WORK, (s + 1) * WORK)
            mask = bias[s]
            parts = []
            for j in range(PIECE_HEADS):
                h = k * PIECE_HEADS + j
                c = slice(h * HEAD_DIM, (h + 1) * HEAD_DIM)
                score = lax.dot_general(q_ref[rows, c], k_ref[rows, c], NT,
                                        preferred_element_type=F32) * (1.0 / ROOT) + mask
                weight = jnp.exp(score - jnp.max(score, axis=1, keepdims=True))
                chance = weight * (1.0 / jnp.sum(weight, axis=1, keepdims=True))
                prob[2 * h + s] = chance
                parts.append(jnp.dot(chance.astype(BF16), v_ref[rows, c],
                                     preferred_element_type=F32))
            parts = jnp.concatenate(parts, axis=1)
            if s == 0:
                att_lo[k] = keep(valid_lo, parts)
            else:
                att_hi[k] = keep(valid_hi, parts)
        att_copy(k).start()

    def span(k):
        return pl.ds(pl.multiple_of(k * PIECE, PIECE), PIECE)

    def ag_up(s, k):
        block = gath.at[s, :, span(k)]
        p = s * sub + k
        return remote(block, block, up_send.at[p], ag_recv.at[p], high)

    def ag_down(s, k):
        block = gath.at[s, :, span(k)]
        p = s * sub + k
        return remote(block, block, down_send.at[p], ag_recv.at[p], low)

    def send_own(k):
        og_copy(k).wait_recv()
        gath[z, :, cols(k)] = jnp.where(own_place, og_ref[0:WORK, cols(k)].astype(F32),
                                        flipped(og_in[k])).astype(BF16)

        @pl.when(has_high)
        def _():
            ag_up(z, k).start()

        @pl.when(has_low)
        def _():
            ag_down(z, k).start()

    def shard_term(c):
        return lax.dot_general(gath[c], w_buf[c], NT, preferred_element_type=F32)

    def gather_item(i):
        d, k = i // sub, lax.rem(i, sub)
        below, above = z - d, z + d

        @pl.when(below >= 0)
        def _():
            ag_up(below, k).wait_recv()

            @pl.when(has_high)
            def _():
                ag_up(below, k).start()

        @pl.when(above < groups)
        def _():
            ag_down(above, k).wait_recv()

            @pl.when(has_low)
            def _():
                ag_down(above, k).start()

    farthest = jnp.maximum(z, groups - 1 - z)

    def gather_add(i):
        d, k = i // sub, lax.rem(i, sub)
        below, above = z - d, z + d

        @pl.when((below >= 0) & (k == sub - 1))
        def _():
            ga_acc[...] += shard_term(below)

        @pl.when((above < groups) & (k == sub - 1))
        def _():
            ga_acc[...] += shard_term(above)

        @pl.when((d == farthest) & (k == sub - 1))
        def _():
            for j in range(sub):
                piece = ga_acc[:, cols(j)].astype(BF16)
                ga_out[j] = piece
                ga_lo[j] = jnp.where(valid_lo, piece.astype(F32), 0.0).astype(BF16)
                ga_copy(j).start()

    def partial(c, k):
        return jnp.dot(att_work[...], w_buf[c, :, span(k)], preferred_element_type=F32)

    def rs_up(p):
        return remote(rs_out.at[p], rs_in.at[p], rs_send.at[p], rs_recv.at[p], high)

    def rs_down(p, slot):
        return remote(rs_out.at[p], rs_in.at[slot], rs_send.at[p], rs_recv.at[slot], low)

    up_end = jnp.where(has_low, (groups - 1 - z) * sub + z, 0)
    down_end = jnp.where(has_high, z * sub + groups - 1 - z, 0)
    end_slot = jnp.maximum(up_end, down_end)

    def scatter_slot(n):
        i = n - z
        c, k = groups - 1 - i // sub, lax.rem(i, sub)

        @pl.when((i >= 0) & (c > z))
        def _():
            p = c * sub + k
            result = partial(c, k)

            @pl.when(has_low)
            def _():
                rs_up(p).wait_recv()
                rs_out[p] = (result + rs_in[p].astype(F32)).astype(BF16)

            @pl.when(jnp.logical_not(has_low))
            def _():
                rs_out[p] = result.astype(BF16)

            rs_up(p).start()

        i2 = n - (groups - 1 - z)
        c2, k2 = i2 // sub, lax.rem(i2, sub)

        @pl.when((i2 >= 0) & (c2 < z))
        def _():
            p = c2 * sub + k2
            result = partial(c2, k2)

            @pl.when(has_high)
            def _():
                rs_down(p, p).wait_recv()
                rs_out[p] = (result + rs_in[p].astype(F32)).astype(BF16)

            @pl.when(jnp.logical_not(has_high))
            def _():
                rs_out[p] = result.astype(BF16)

            slot = jnp.where(c2 == z - 1, total + k2, p)
            rs_down(p, slot).start()

        k3 = n - end_slot

        @pl.when((k3 >= 0) & (k3 < sub))
        def _():
            scatter_end(k3)

    def scatter_end(k):
        p = z * sub + k
        pr_acc[...] = partial(z, k)

        @pl.when(has_low)
        def _():
            rs_up(p).wait_recv()
            pr_acc[...] += rs_in[p].astype(F32)

        @pl.when(has_high)
        def _():
            rs_down(p, total + k).wait_recv()
            pr_acc[...] += rs_in[total + k].astype(F32)

        pr_work[k] = pr_acc[...].astype(BF16)
        pr_copy(k).start()

    def backward(k, s, grads):
        rows = slice(s * WORK, (s + 1) * WORK)
        valid = (valid_lo if s == 0 else valid_hi)[:, 0:HEAD_DIM]
        for j in range(PIECE_HEADS):
            h = k * PIECE_HEADS + j
            c = pl.ds(pl.multiple_of(h * HEAD_DIM, HEAD_DIM), HEAD_DIM)
            chance = prob[2 * h + s]
            grad = grads[:, j * HEAD_DIM:(j + 1) * HEAD_DIM]
            gv = lax.dot_general(chance.astype(BF16), grad, TN, preferred_element_type=F32)
            gw = lax.dot_general(grad, v_ref[rows, c], NT, preferred_element_type=F32)
            correction = jnp.sum(chance * gw, axis=1, keepdims=True)
            gs = (chance * (gw - correction) * (1.0 / ROOT)).astype(BF16)
            gq = jnp.dot(gs, k_ref[rows, c], preferred_element_type=F32)
            gk = lax.dot_general(gs, q_ref[rows, c], TN, preferred_element_type=F32)
            gv_ref[rows, c] = keep(valid, gv)
            gq_ref[rows, c] = keep(valid, gq)
            gk_ref[rows, c] = keep(valid, gk)

    def results(s, first, last):
        rows = pl.ds(s * WORK, WORK)
        return [
            pltpu.make_async_copy(held.at[rows, :], target.at[rows, :], out_sem.at[2 * n + s])
            for n, (held, target) in enumerate(
                [(gq_ref, gq_out), (gk_ref, gk_out), (gv_ref, gv_out), (proj_ref, proj_out)]
            )
            if first <= n < last
        ]

    for load in loads:
        load.wait()
    for k in range(sub):
        forward(k)
        if k == 0:
            for later in range(1, early):
                og_copy(later).start()
            send_own(0)
    for k in range(early, sub):
        og_copy(k).start()
    for k in range(1, early):
        send_own(k)
    for k in range(early):
        gather_item(jnp.int32(sub + k))

    @pl.loop(0, groups)
    def _(c):
        w_copy(c).wait()

    steps = (groups - 1) * sub
    for k in range(sub):
        att_copy(k).wait_recv()
        att_work[:, cols(k)] = jnp.where(own_place, att_lo[k].astype(F32),
                                         flipped(att_in[k])).astype(BF16)
        if k < early - 1:
            gather_item(jnp.int32(2 * sub + k))
    scatter_slot(jnp.int32(0))
    for k in range(early, sub):
        send_own(k)
    gather_item(jnp.int32(2 * sub + early - 1))
    scatter_slot(jnp.int32(1))
    for k in range(early, sub):
        gather_item(jnp.int32(sub + k))
    scatter_slot(jnp.int32(2))
    ga_acc[...] = shard_term(z)
    gather_add(jnp.int32(2 * sub - 1))
    for k in range(early, sub):
        gather_item(jnp.int32(2 * sub + k))
    gather_add(jnp.int32(3 * sub - 1))
    ahead = 3

    @pl.loop(0, steps - 2 * sub)
    def _(n):
        scatter_slot(n + ahead)
        gather_item(n + 3 * sub)
        gather_add(n + 3 * sub)

    ahead += steps - 2 * sub

    @pl.loop(0, sub)
    def _(k):
        @pl.when(k < sub - 1)
        def _():
            scatter_slot(k + ahead)

        backward(k, 0, ga_lo[k])

    ahead += sub - 1
    for copy in results(0, 0, 3):
        copy.start()

    @pl.loop(0, sub)
    def _(k):
        @pl.when(k < sub - 1)
        def _():
            scatter_slot(k + ahead)

        ga_copy(k).wait_recv()
        backward(k, 1, keep(valid_hi, flipped(ga_in[k])))

    for copy in results(1, 0, 3):
        copy.start()

    for k in range(sub):
        pr_copy(k).wait_recv()
        proj_ref[0:WORK, cols(k)] = keep(valid_lo, pr_work[k].astype(F32))
        proj_ref[WORK:2 * WORK, cols(k)] = keep(valid_hi, flipped(pr_in[k]))
    for s in range(2):
        results(s, 3, 4)[0].start()

    for k in range(sub):
        og_copy(k).wait_send()
        att_copy(k).wait_send()
        ga_copy(k).wait_send()
        pr_copy(k).wait_send()

    @pl.loop(0, total)
    def _(p):
        c, k = p // sub, lax.rem(p, sub)

        @pl.when(has_high & (c <= z))
        def _():
            ag_up(c, k).wait_send()

        @pl.when(has_low & (c >= z))
        def _():
            ag_down(c, k).wait_send()

        @pl.when(c != z)
        def _():
            rs_up(p).wait_send()

    for s in range(2):
        for copy in results(s, 0, 4):
            copy.wait()


def hand_over(*refs):
    sources, targets, (held, in_sem, out_sem) = refs[:4], refs[4:8], refs[8:]
    half = sources[0].shape[0] // 2
    loads, stores = [], []
    for s in range(2):
        rows = pl.ds(s * half, half)
        for n in range(4):
            spot = held.at[n, rows, :]
            loads.append(pltpu.make_async_copy(sources[n].at[rows, :], spot, in_sem.at[n, s]))
            stores.append(pltpu.make_async_copy(spot, targets[n].at[rows, :], out_sem.at[n, s]))
    for load in loads:
        load.start()
    for load, store in zip(loads, stores):
        load.wait()
        store.start()
    for store in stores:
        store.wait()


def solution(mesh):
    packs, groups = mesh.shape["dp"], mesh.shape["mp"]

    def shards(query_rows, key_rows, value_rows, proj_weight, out_grad, image_starts):
        rows, width = query_rows.shape
        piece = piece_width(width)
        sub = width // piece
        total = groups * sub
        vmem = pl.BlockSpec(memory_space=pltpu.VMEM)
        anywhere = pl.BlockSpec(memory_space=pl.ANY)
        dma = pltpu.SemaphoreType.DMA
        block = jax.ShapeDtypeStruct((rows, width), BF16)

        def pieces(count):
            return pltpu.VMEM((count, WORK, piece), BF16)

        results = pl.pallas_call(
            functools.partial(kernel, packs, groups),
            out_shape=(block,) * 4,
            in_specs=[anywhere] * 4 + [vmem, anywhere],
            out_specs=(anywhere,) * 4,
            scratch_shapes=[pltpu.VMEM((rows, width), BF16)] * 8 + [
                pltpu.VMEM((2, WORK, WORK), F32),
                pltpu.VMEM((groups, width, width), BF16),
                pltpu.VMEM((2 * width // HEAD_DIM, WORK, WORK), F32),
                pieces(sub), pieces(sub), pieces(sub),
                pltpu.VMEM((WORK, width), BF16),
                pieces(sub),
                pltpu.VMEM((groups, WORK, width), BF16),
                pltpu.VMEM((WORK, width), F32),
                pltpu.VMEM((WORK, piece), F32),
                pieces(sub), pieces(sub), pieces(sub),
                pieces(total + sub), pieces(total),
                pieces(sub), pieces(sub),
                dma((4,)), dma((8,)), dma((groups,)),
                dma((sub,)), dma((sub,)), dma((sub,)), dma((sub,)),
                dma((sub,)), dma((sub,)), dma((sub,)), dma((sub,)),
                dma((total,)), dma((total,)), dma((total,)),
                dma((total,)), dma((total + sub,)),
            ],
            compiler_params=pltpu.CompilerParams(
                collective_id=0, has_side_effects=True, vmem_limit_bytes=56 * 2**20
            ),
            cost_estimate=pl.CostEstimate(
                flops=4 * WORK * width * width * groups,
                bytes_accessed=2 * width * width * groups + 16 * rows * width,
                transcendentals=rows * width,
            ),
        )(query_rows, key_rows, value_rows, out_grad, image_starts, proj_weight)
        return pl.pallas_call(
            hand_over,
            out_shape=(block,) * 4,
            in_specs=[anywhere] * 4,
            out_specs=(anywhere,) * 4,
            scratch_shapes=[pltpu.VMEM((4, rows, width), BF16), dma((4, 2)), dma((4, 2))],
            compiler_params=pltpu.CompilerParams(vmem_limit_bytes=60 * 2**20),
        )(*results)

    placed = (P("dp", "mp"), P("dp", "mp"), P("dp", "mp"), P("mp", None), P("dp", "mp"), P())
    return jax.shard_map(
        shards,
        mesh=mesh,
        in_specs=placed,
        out_specs=(P("dp", "mp"), P("dp", "mp"), P("dp", "mp"), P("dp", "mp")),
        check_vma=False,
    )
```
